32 devices in a mesh: groups: 2 (over y), segment: 2 (over core), seq: 8 (over z, x).
Axes of the slice: x: 2, y: 2, z: 4, core: 2. Of those that a mesh axis runs over, the one named last changes fastest.
Arguments:
- held: bfloat16 [2, 32, 8, 16, 640], P('segment', ('groups', 'seq')), parts along dimension 1, may hold values from -6 to 6
- arrivals: bfloat16 [3, 32, 8, 16, 640], P(None, ('groups', 'seq')), parts along dimension 1, may hold values from -6 to 6
- spatial_weight: bfloat16 [2, 9, 640, 640], P('segment'), may hold values from -0.078125 to 0.078125
- spatial_scale: float32 [2, 5, 640], P('segment'), may hold values from 0.5 to 2
- temporal_weight: bfloat16 [2, 3, 640, 640], P('segment'), may hold values from -0.125 to 0.125
- temporal_scale: float32 [2, 5, 640], P('segment'), may hold values from 0.5 to 2
Outputs:
- emitted: bfloat16 [2, 4, 32, 8, 16, 640], P('segment', None, ('groups', 'seq')), parts along dimension 2
The draws below stay inside these ranges and needn't reach their ends.
There are 2 independent parts, one for each index of `groups`. The reference program is written for one: setup_inputs(seed, part) draws one part's arguments, and reference() takes and returns one part's arrays. A program takes and returns all parts, laid end to end along the dimension named above; an argument that names none is the same for every part. Nothing has to cross between parts.
All inputs are finite; a program needn't handle non-finite values.
Results may differ from the reference program's by a relative error of at most 0.014.
Values may be sent and summed in bfloat16 or wider, within the bound.
A program may use at most 128 MiB of HBM per device.

```python
import math
import jax
import jax.numpy as jnp

C = 640
BLOCK = 128
H = 8
W = 16
TICKS = 4
SECTIONS = 2
FRAMES = 16
N_SEGMENT = 2


def block_levels(stream_key, dims, shards, least, top_value):
    level, own = 1.0, jax.random.fold_in(stream_key, 6)
    for dim, blocks in shards:
        steps = jnp.exp(jax.random.uniform(jax.random.fold_in(own, dim), (blocks,), jnp.float32, least / len(shards), top_value / len(shards)))
        level = level * jnp.repeat(steps, dims[dim] // blocks).reshape([-1 if axis == dim else 1 for axis in range(len(dims))])
    return level


def centred(key, extent, spread, reach, split=(), kind=jnp.bfloat16):
    array = spread * jax.random.normal(key, extent, jnp.float32)
    if split:
        array = array * block_levels(key, extent, split, -0.22, 0.18)
    return jnp.clip(array, -reach, reach).astype(kind)


def setup_inputs(seed: int = 0, part: int = 0) -> dict:
    key_list = jax.random.split(jax.random.key(seed), 7)
    own_keys = jax.random.split(jax.random.fold_in(key_list[6], part), 7)
    held = centred(own_keys[0], (N_SEGMENT, FRAMES, H, W, C), 1.0, 6.0, ((0, 2), (1, 8)))
    arrivals = centred(own_keys[1], (TICKS - 1, FRAMES, H, W, C), 1.0, 6.0, ((1, 8),))
    spatial_weight = centred(key_list[2], (SECTIONS, 9, C, C), (9 * C) ** -0.5, 0.078125, ((0, 2),))
    spatial_scale = jnp.clip(jnp.exp(math.log(2.0) - 1.3862944 * jax.random.uniform(key_list[3], (SECTIONS, C // BLOCK, C), jnp.float32) ** block_levels(key_list[3], (SECTIONS, C // BLOCK, C), ((0, 2),), -0.2, 0.2)), 0.5, 2.0)
    temporal_weight = centred(key_list[4], (SECTIONS, 3, C, C), (3 * C) ** -0.5, 0.125, ((0, 2),))
    temporal_scale = jnp.clip(jnp.exp(math.log(2.0) - 1.3862944 * jax.random.uniform(key_list[5], (SECTIONS, C // BLOCK, C), jnp.float32) ** block_levels(key_list[5], (SECTIONS, C // BLOCK, C), ((0, 2),), -0.2, 0.2)), 0.5, 2.0)
    return dict(held=held, arrivals=arrivals, spatial_weight=spatial_weight, spatial_scale=spatial_scale, temporal_weight=temporal_weight, temporal_scale=temporal_scale)


def dequantize(weights, scales):
    block = weights.shape[1] // scales.shape[0]
    expanded = jnp.repeat(scales, block, axis=0)
    return (weights.astype(jnp.float32) * expanded[None]).astype(jnp.bfloat16)


def spatial_term(activation, kernels):
    frames, height, width, channels = activation.shape
    padded = jnp.pad(activation, ((0, 0), (1, 1), (1, 1), (0, 0)))
    total = jnp.zeros((frames * height * width, channels), jnp.float32)
    for row_tap in range(3):
        for col_tap in range(3):
            window = padded[:, row_tap:row_tap + height, col_tap:col_tap + width].reshape(-1, channels)
            total = total + jnp.dot(window, kernels[row_tap * 3 + col_tap], preferred_element_type=jnp.float32)
    return total.reshape(activation.shape)


def temporal_term(activation, kernels):
    frames = activation.shape[0]
    channels = activation.shape[-1]
    blank = jnp.zeros((1,) + activation.shape[1:], activation.dtype)
    padded = jnp.concatenate([blank, activation, blank], axis=0)
    total = jnp.zeros((activation.size // channels, channels), jnp.float32)
    for frame_tap in range(3):
        window = padded[frame_tap:frame_tap + frames].reshape(-1, channels)
        total = total + jnp.dot(window, kernels[frame_tap], preferred_element_type=jnp.float32)
    return total.reshape(activation.shape).astype(jnp.bfloat16)


def section(activation, spatial_kernels, temporal_kernels):
    lifted = jax.nn.silu(activation.astype(jnp.float32)).astype(jnp.bfloat16)
    middle = (activation.astype(jnp.float32) + spatial_term(lifted, spatial_kernels)).astype(jnp.bfloat16)
    lifted_mid = jax.nn.silu(middle.astype(jnp.float32)).astype(jnp.bfloat16)
    temporal = temporal_term(lifted_mid, temporal_kernels)
    return (middle.astype(jnp.float32) + temporal.astype(jnp.float32)).astype(jnp.bfloat16)


def reference(held, arrivals, spatial_weight, spatial_scale, temporal_weight, temporal_scale):
    segments = held.shape[0]
    per_segment = spatial_weight.shape[0] // segments
    ticks = arrivals.shape[0] + 1
    spatial_kernels = [dequantize(spatial_weight[k], spatial_scale[k]) for k in range(spatial_weight.shape[0])]
    temporal_kernels = [dequantize(temporal_weight[k], temporal_scale[k]) for k in range(temporal_weight.shape[0])]
    inputs = [held[segment_index] for segment_index in range(segments)]
    collected = [[] for segment_index in range(segments)]
    for tick_index in range(ticks):
        outputs = []
        for segment_index in range(segments):
            current = inputs[segment_index]
            for inner in range(per_segment):
                number = segment_index * per_segment + inner
                current = section(current, spatial_kernels[number], temporal_kernels[number])
            outputs.append(current)
            collected[segment_index].append(current)
        if tick_index + 1 < ticks:
            inputs = [arrivals[tick_index]] + outputs[:-1]
    return jnp.stack([jnp.stack(series) for series in collected])
```

```python
import functools

import jax
import jax.numpy as jnp
from jax import lax
from jax.experimental import pallas as pl
from jax.experimental.pallas import tpu as pltpu
from jax.sharding import PartitionSpec as P

MESH = pl.DeviceIdType.MESH


def silu(v):
    return v / (1.0 + jnp.exp(-v))


def kernel(
    n_segment, n_seq,
    held, arrivals, w_s, s_s, w_t, s_t, out,
    clips, padded, ks, kt, middle, ext, results,
    clip_sem, ks_sem, kt_sem, out_sem, relay_send, relay_recv, halo_send, halo_recv,
):
    ticks, frames, height, width, channels = clips.shape
    rows = frames * height * width
    segment, seq = lax.axis_index("segment"), lax.axis_index("seq")
    has_left, has_right = seq > 0, seq < n_seq - 1
    has_up, has_down = segment > 0, segment < n_segment - 1
    neighbours = (
        (has_left, {"seq": seq - 1}),
        (has_right, {"seq": seq + 1}),
        (has_up, {"segment": segment - 1}),
        (has_down, {"segment": segment + 1}),
    )
    barrier = pltpu.get_barrier_semaphore()
    for there, where in neighbours:
        @pl.when(there)
        def _(where=where):
            pl.semaphore_signal(barrier, inc=1, device_id=where, device_id_type=MESH)

    def load_held():
        return pltpu.make_async_copy(held.at[0], clips.at[0], clip_sem.at[0])

    def load_arrival(t):
        return pltpu.make_async_copy(arrivals.at[t - 1], clips.at[t], clip_sem.at[t])

    def load_ks(row):
        return pltpu.make_async_copy(w_s.at[0, pl.ds(3 * row, 3)], ks.at[pl.ds(3 * row, 3)], ks_sem.at[row])

    def load_kt():
        return pltpu.make_async_copy(w_t.at[0], kt, kt_sem)

    def store(t):
        return pltpu.make_async_copy(results.at[t], out.at[0, t], out_sem.at[t])

    def relay(t):
        return pltpu.make_async_remote_copy(
            results.at[t], clips.at[t + 1], relay_send.at[t], relay_recv.at[t],
            device_id={"segment": segment + 1}, device_id_type=MESH,
        )

    def tail(t):
        return pltpu.make_async_remote_copy(
            ext.at[t, frames], ext.at[t, 0], halo_send.at[t, 0], halo_recv.at[t, 0],
            device_id={"seq": seq + 1}, device_id_type=MESH,
        )

    def head(t):
        return pltpu.make_async_remote_copy(
            ext.at[t, 1], ext.at[t, frames + 1], halo_send.at[t, 1], halo_recv.at[t, 1],
            device_id={"seq": seq - 1}, device_id_type=MESH,
        )

    load_held().start()
    for row in range(3):
        load_ks(row).start()
    load_kt().start()

    @pl.when(segment == 0)
    def _():
        for t in range(1, ticks):
            load_arrival(t).start()

    blank = jnp.zeros((frames, 1, width, 3 * channels), jnp.bfloat16)
    padded[:, 0:1] = blank
    padded[:, height + 1 : height + 2] = blank

    @pl.when(jnp.logical_not(has_left))
    def _():
        ext[:, 0] = jnp.zeros((ticks, height, width, channels), jnp.bfloat16)

    @pl.when(jnp.logical_not(has_right))
    def _():
        ext[:, frames + 1] = jnp.zeros((ticks, height, width, channels), jnp.bfloat16)

    def scale(kernels, tap, scales):
        blocks = scales.shape[1]
        block = channels // blocks
        for i in range(blocks):
            part = slice(i * block, (i + 1) * block)
            kernels[tap, part, :] = (
                kernels[tap, part, :].astype(jnp.float32) * scales[0, i : i + 1, :]
            ).astype(jnp.bfloat16)

    def spatial(t, first):
        x = clips[t].reshape(rows, channels).astype(jnp.float32)
        lifted = silu(x)
        column = lax.broadcasted_iota(jnp.int32, (rows, channels), 0) % width
        before = jnp.where(column == 0, 0.0, pltpu.roll(lifted, 1, 0))
        after = jnp.where(column == width - 1, 0.0, pltpu.roll(lifted, rows - 1, 0))
        for b, part in enumerate((before, lifted, after)):
            padded[:, 1 : height + 1, :, b * channels : (b + 1) * channels] = part.astype(
                jnp.bfloat16
            ).reshape(frames, height, width, channels)
        total = x
        for a in range(3):
            if first:
                load_ks(a).wait()
                for b in range(3):
                    scale(ks, 3 * a + b, s_s)
            total = total + jnp.dot(
                padded[:, a : a + height].reshape(rows, 3 * channels),
                ks[3 * a : 3 * a + 3].reshape(3 * channels, channels),
                preferred_element_type=jnp.float32,
            )
        mid = total.astype(jnp.bfloat16)
        middle[t] = mid
        ext[t, 1 : frames + 1] = silu(mid.astype(jnp.float32)).astype(jnp.bfloat16).reshape(
            frames, height, width, channels
        )

    def send_halo(t):
        @pl.when(has_right)
        def _():
            tail(t).start()

        @pl.when(has_left)
        def _():
            head(t).start()

    def temporal(t):
        @pl.when(has_left)
        def _():
            tail(t).wait_recv()

        @pl.when(has_right)
        def _():
            head(t).wait_recv()

        total = jnp.zeros((rows, channels), jnp.float32)
        for j in range(3):
            total = total + jnp.dot(
                ext[t, j : j + frames].reshape(rows, channels), kt[j],
                preferred_element_type=jnp.float32,
            )
        results[t] = (
            middle[t].astype(jnp.float32) + total.astype(jnp.bfloat16).astype(jnp.float32)
        ).astype(jnp.bfloat16).reshape(frames, height, width, channels)
        store(t).start()

    load_held().wait()
    spatial(0, True)
    pl.semaphore_wait(barrier, sum(there.astype(jnp.int32) for there, _ in neighbours))
    send_halo(0)
    load_kt().wait()
    for j in range(3):
        scale(kt, j, s_t)

    def step(t, carry):
        @pl.when(segment == 0)
        def _():
            load_arrival(t).wait()

        @pl.when(has_up)
        def _():
            relay(t - 1).wait_recv()

        spatial(t, False)
        send_halo(t)
        temporal(t - 1)

        @pl.when(has_down)
        def _():
            relay(t - 1).start()

        return carry

    lax.fori_loop(1, ticks, step, 0)
    temporal(ticks - 1)

    for t in range(ticks):
        store(t).wait()

        @pl.when(has_right)
        def _(t=t):
            tail(t).wait_send()

        @pl.when(has_left)
        def _(t=t):
            head(t).wait_send()

        if t < ticks - 1:
            @pl.when(has_down)
            def _(t=t):
                relay(t).wait_send()


def local(n_segment, n_seq, held, arrivals, w_s, s_s, w_t, s_t):
    ticks = arrivals.shape[0] + 1
    _, frames, height, width, channels = held.shape
    clip = (frames, height, width, channels)
    bf16, dma = jnp.bfloat16, pltpu.SemaphoreType.DMA
    hbm, vmem = pl.BlockSpec(memory_space=pl.ANY), pl.BlockSpec(memory_space=pltpu.VMEM)
    rows = frames * height * width
    return pl.pallas_call(
        functools.partial(kernel, n_segment, n_seq),
        out_shape=jax.ShapeDtypeStruct((1, ticks) + clip, bf16),
        in_specs=[hbm, hbm, hbm, vmem, hbm, vmem],
        out_specs=hbm,
        scratch_shapes=[
            pltpu.VMEM((ticks,) + clip, bf16),
            pltpu.VMEM((frames, height + 2, width, 3 * channels), bf16),
            pltpu.VMEM(w_s.shape[1:], bf16),
            pltpu.VMEM(w_t.shape[1:], bf16),
            pltpu.VMEM((ticks, rows, channels), bf16),
            pltpu.VMEM((ticks, frames + 2, height, width, channels), bf16),
            pltpu.VMEM((ticks,) + clip, bf16),
            dma((ticks,)), dma((3,)), dma, dma((ticks,)),
            dma((ticks,)), dma((ticks,)), dma((ticks, 2)), dma((ticks, 2)),
        ],
        compiler_params=pltpu.CompilerParams(
            collective_id=0, has_side_effects=True, vmem_limit_bytes=48 * 2**20
        ),
        cost_estimate=pl.CostEstimate(
            flops=2 * ticks * 12 * rows * channels * channels, bytes_accessed=2 * (w_s.size + w_t.size),
            transcendentals=0,
        ),
    )(held, arrivals, w_s, s_s, w_t, s_t)


def solution(mesh):
    in_specs = (
        P("segment", ("groups", "seq"), None, None, None),
        P(None, ("groups", "seq"), None, None, None),
        P("segment", None, None, None),
        P("segment", None, None),
        P("segment", None, None, None),
        P("segment", None, None),
    )
    out_specs = P("segment", None, ("groups", "seq"), None, None, None)
    body = functools.partial(local, mesh.shape["segment"], mesh.shape["seq"])
    return jax.shard_map(body, mesh=mesh, in_specs=in_specs, out_specs=out_specs, check_vma=False)
```

```python
import functools

import jax
import jax.numpy as jnp
from jax import lax
from jax.experimental import pallas as pl
from jax.experimental.pallas import tpu as pltpu
from jax.sharding import PartitionSpec as P

MESH = pl.DeviceIdType.MESH


def silu(v):
    return v / (1.0 + jnp.exp(-v))


def kernel(
    n_segment, n_seq,
    held, arrivals, w_s, s_s, w_t, s_t, out,
    clips, padded, ks, kt, middle, ext, results,
    clip_sem, ks_sem, kt_sem, out_sem, relay_send, relay_recv, halo_send, halo_recv,
):
    ticks, frames, height, width, channels = clips.shape
    rows = frames * height * width
    segment, seq = lax.axis_index("segment"), lax.axis_index("seq")
    has_left, has_right = seq > 0, seq < n_seq - 1
    has_up, has_down = segment > 0, segment < n_segment - 1
    neighbours = (
        (has_left, {"seq": seq - 1}),
        (has_right, {"seq": seq + 1}),
        (has_up, {"segment": segment - 1}),
        (has_down, {"segment": segment + 1}),
    )
    barrier = pltpu.get_barrier_semaphore()
    for there, where in neighbours:
        @pl.when(there)
        def _(where=where):
            pl.semaphore_signal(barrier, inc=1, device_id=where, device_id_type=MESH)

    def load_held():
        return pltpu.make_async_copy(held.at[0], clips.at[0], clip_sem.at[0])

    def load_arrival(t):
        return pltpu.make_async_copy(arrivals.at[t - 1], clips.at[t], clip_sem.at[t])

    def load_ks(row):
        return pltpu.make_async_copy(w_s.at[0, pl.ds(3 * row, 3)], ks.at[pl.ds(3 * row, 3)], ks_sem.at[row])

    def load_kt():
        return pltpu.make_async_copy(w_t.at[0], kt, kt_sem)

    def store(t):
        return pltpu.make_async_copy(results.at[t], out.at[0, t], out_sem.at[t])

    def relay(t):
        return pltpu.make_async_remote_copy(
            results.at[t], clips.at[t + 1], relay_send.at[t], relay_recv.at[t],
            device_id={"segment": segment + 1}, device_id_type=MESH,
        )

    def tail(t):
        return pltpu.make_async_remote_copy(
            ext.at[t, frames], ext.at[t, 0], halo_send.at[t, 0], halo_recv.at[t, 0],
            device_id={"seq": seq + 1}, device_id_type=MESH,
        )

    def head(t):
        return pltpu.make_async_remote_copy(
            ext.at[t, 1], ext.at[t, frames + 1], halo_send.at[t, 1], halo_recv.at[t, 1],
            device_id={"seq": seq - 1}, device_id_type=MESH,
        )

    load_held().start()
    for row in range(3):
        load_ks(row).start()
    load_kt().start()

    @pl.when(segment == 0)
    def _():
        for t in range(1, ticks):
            load_arrival(t).start()

    blank = jnp.zeros((frames, 1, width, 3 * channels), jnp.bfloat16)
    padded[:, 0:1] = blank
    padded[:, height + 1 : height + 2] = blank

    @pl.when(jnp.logical_not(has_left))
    def _():
        ext[:, 0] = jnp.zeros((ticks, height, width, channels), jnp.bfloat16)

    @pl.when(jnp.logical_not(has_right))
    def _():
        ext[:, frames + 1] = jnp.zeros((ticks, height, width, channels), jnp.bfloat16)

    def scale(kernels, tap, scales):
        blocks = scales.shape[0]
        block = channels // blocks
        for i in range(blocks):
            part = slice(i * block, (i + 1) * block)
            kernels[tap, part, :] = (
                kernels[tap, part, :].astype(jnp.float32) * scales[i]
            ).astype(jnp.bfloat16)

    def spatial(t, first):
        x = clips[t].reshape(rows, channels).astype(jnp.float32)
        lifted = silu(x)
        column = lax.broadcasted_iota(jnp.int32, (rows, channels), 0) % width
        before = jnp.where(column == 0, 0.0, pltpu.roll(lifted, 1, 0))
        after = jnp.where(column == width - 1, 0.0, pltpu.roll(lifted, rows - 1, 0))
        for b, part in enumerate((before, lifted, after)):
            padded[:, 1 : height + 1, :, b * channels : (b + 1) * channels] = part.astype(
                jnp.bfloat16
            ).reshape(frames, height, width, channels)
        total = x
        for a in range(3):
            if first:
                load_ks(a).wait()
                for b in range(3):
                    scale(ks, 3 * a + b, s_s)
            total = total + jnp.dot(
                padded[:, a : a + height].reshape(rows, 3 * channels),
                ks[3 * a : 3 * a + 3].reshape(3 * channels, channels),
                preferred_element_type=jnp.float32,
            )
        mid = total.astype(jnp.bfloat16)
        middle[t] = mid
        ext[t, 1 : frames + 1] = silu(mid.astype(jnp.float32)).astype(jnp.bfloat16).reshape(
            frames, height, width, channels
        )

    def send_halo(t):
        @pl.when(has_right)
        def _():
            tail(t).start()

        @pl.when(has_left)
        def _():
            head(t).start()

    def temporal(t):
        @pl.when(has_left)
        def _():
            tail(t).wait_recv()

        @pl.when(has_right)
        def _():
            head(t).wait_recv()

        total = jnp.zeros((rows, channels), jnp.float32)
        for j in range(3):
            total = total + jnp.dot(
                ext[t, j : j + frames].reshape(rows, channels), kt[j],
                preferred_element_type=jnp.float32,
            )
        results[t] = (
            middle[t].astype(jnp.float32) + total.astype(jnp.bfloat16).astype(jnp.float32)
        ).astype(jnp.bfloat16).reshape(frames, height, width, channels)
        store(t).start()

    load_held().wait()
    spatial(0, True)
    pl.semaphore_wait(barrier, sum(there.astype(jnp.int32) for there, _ in neighbours))

    @pl.when(segment == 0)
    def _():
        send_halo(0)

    load_kt().wait()
    for j in range(3):
        scale(kt, j, s_t)

    def step(t, carry):
        @pl.when(segment == 0)
        def _():
            load_arrival(t).wait()

        @pl.when(has_up)
        def _():
            relay(t - 1).wait_recv()

            @pl.when(t == 1)
            def _():
                send_halo(0)

        spatial(t, False)
        send_halo(t)
        temporal(t - 1)

        @pl.when(has_down)
        def _():
            relay(t - 1).start()

        return carry

    lax.fori_loop(1, ticks, step, 0)
    temporal(ticks - 1)

    for t in range(ticks):
        store(t).wait()

        @pl.when(has_right)
        def _(t=t):
            tail(t).wait_send()

        @pl.when(has_left)
        def _(t=t):
            head(t).wait_send()

        if t < ticks - 1:
            @pl.when(has_down)
            def _(t=t):
                relay(t).wait_send()


def local(n_segment, n_seq, held, arrivals, w_s, s_s, w_t, s_t):
    ticks = arrivals.shape[0] + 1
    _, frames, height, width, channels = held.shape
    clip = (frames, height, width, channels)
    bf16, dma = jnp.bfloat16, pltpu.SemaphoreType.DMA
    hbm, vmem = pl.BlockSpec(memory_space=pl.ANY), pl.BlockSpec(memory_space=pltpu.VMEM)
    rows = frames * height * width
    return pl.pallas_call(
        functools.partial(kernel, n_segment, n_seq),
        out_shape=jax.ShapeDtypeStruct((1, ticks) + clip, bf16),
        in_specs=[hbm, hbm, hbm, vmem, hbm, vmem],
        out_specs=hbm,
        scratch_shapes=[
            pltpu.VMEM((ticks,) + clip, bf16),
            pltpu.VMEM((frames, height + 2, width, 3 * channels), bf16),
            pltpu.VMEM(w_s.shape[1:], bf16),
            pltpu.VMEM(w_t.shape[1:], bf16),
            pltpu.VMEM((ticks, rows, channels), bf16),
            pltpu.VMEM((ticks, frames + 2, height, width, channels), bf16),
            pltpu.VMEM((ticks,) + clip, bf16),
            dma((ticks,)), dma((3,)), dma, dma((ticks,)),
            dma((ticks,)), dma((ticks,)), dma((ticks, 2)), dma((ticks, 2)),
        ],
        compiler_params=pltpu.CompilerParams(
            collective_id=0, has_side_effects=True, vmem_limit_bytes=60 * 2**20
        ),
        cost_estimate=pl.CostEstimate(
            flops=2 * ticks * 12 * rows * channels * channels, bytes_accessed=2 * (w_s.size + w_t.size),
            transcendentals=0,
        ),
    )(held, arrivals, w_s, jnp.swapaxes(s_s, 0, 1), w_t, jnp.swapaxes(s_t, 0, 1))


def solution(mesh):
    in_specs = (
        P("segment", ("groups", "seq"), None, None, None),
        P(None, ("groups", "seq"), None, None, None),
        P("segment", None, None, None),
        P("segment", None, None),
        P("segment", None, None, None),
        P("segment", None, None),
    )
    out_specs = P("segment", None, ("groups", "seq"), None, None, None)
    body = functools.partial(local, mesh.shape["segment"], mesh.shape["seq"])
    return jax.shard_map(body, mesh=mesh, in_specs=in_specs, out_specs=out_specs, check_vma=False)
```

```python
import functools

import jax
import jax.numpy as jnp
from jax import lax
from jax.experimental import pallas as pl
from jax.experimental.pallas import tpu as pltpu
from jax.sharding import PartitionSpec as P

MESH = pl.DeviceIdType.MESH


def silu(v):
    return v / (1.0 + jnp.exp(-v))


def kernel(
    n_segment, n_seq,
    held, arrivals, w_s, s_s, w_t, s_t, out,
    clips, padded, ks, kt, middle, ext, results,
    clip_sem, ks_sem, kt_sem, out_sem, relay_send, relay_recv, halo_send, halo_recv,
):
    ticks, frames, height, width, channels = clips.shape
    rows = frames * height * width
    segment, seq = lax.axis_index("segment"), lax.axis_index("seq")
    has_left, has_right = seq > 0, seq < n_seq - 1
    has_up, has_down = segment > 0, segment < n_segment - 1
    neighbours = (
        (has_left, {"seq": seq - 1}),
        (has_right, {"seq": seq + 1}),
        (has_up, {"segment": segment - 1}),
        (has_down, {"segment": segment + 1}),
    )
    barrier = pltpu.get_barrier_semaphore()
    for there, where in neighbours:
        @pl.when(there)
        def _(where=where):
            pl.semaphore_signal(barrier, inc=1, device_id=where, device_id_type=MESH)

    def load_held():
        return pltpu.make_async_copy(held.at[0], clips.at[0], clip_sem.at[0])

    def load_arrival(t):
        return pltpu.make_async_copy(arrivals.at[t - 1], clips.at[t], clip_sem.at[t])

    def load_ks(row):
        return pltpu.make_async_copy(w_s.at[0, pl.ds(3 * row, 3)], ks.at[pl.ds(3 * row, 3)], ks_sem.at[row])

    def load_kt():
        return pltpu.make_async_copy(w_t.at[0], kt, kt_sem)

    def store(t):
        return pltpu.make_async_copy(results.at[t], out.at[0, t], out_sem.at[t])

    def relay(t):
        return pltpu.make_async_remote_copy(
            results.at[t], clips.at[t + 1], relay_send.at[t], relay_recv.at[t],
            device_id={"segment": segment + 1}, device_id_type=MESH,
        )

    def tail(t):
        return pltpu.make_async_remote_copy(
            ext.at[t, frames], ext.at[t, 0], halo_send.at[t, 0], halo_recv.at[t, 0],
            device_id={"seq": seq + 1}, device_id_type=MESH,
        )

    def head(t):
        return pltpu.make_async_remote_copy(
            ext.at[t, 1], ext.at[t, frames + 1], halo_send.at[t, 1], halo_recv.at[t, 1],
            device_id={"seq": seq - 1}, device_id_type=MESH,
        )

    load_held().start()
    for row in range(3):
        load_ks(row).start()
    load_kt().start()

    @pl.when(segment == 0)
    def _():
        for t in range(1, ticks):
            load_arrival(t).start()

    blank = jnp.zeros((frames, 1, width, 3 * channels), jnp.bfloat16)
    padded[:, 0:1] = blank
    padded[:, height + 1 : height + 2] = blank

    @pl.when(jnp.logical_not(has_left))
    def _():
        ext[:, 0] = jnp.zeros((ticks, height, width, channels), jnp.bfloat16)

    @pl.when(jnp.logical_not(has_right))
    def _():
        ext[:, frames + 1] = jnp.zeros((ticks, height, width, channels), jnp.bfloat16)

    def scale(kernels, tap, scales):
        blocks = scales.shape[0]
        block = channels // blocks
        for i in range(blocks):
            part = slice(i * block, (i + 1) * block)
            kernels[tap, part, :] = (
                kernels[tap, part, :].astype(jnp.float32) * scales[i]
            ).astype(jnp.bfloat16)

    def spatial(t, first):
        x = clips[t].reshape(rows, channels).astype(jnp.float32)
        lifted = silu(x)
        column = lax.broadcasted_iota(jnp.int32, (rows, channels), 0) % width
        before = jnp.where(column == 0, 0.0, pltpu.roll(lifted, 1, 0))
        after = jnp.where(column == width - 1, 0.0, pltpu.roll(lifted, rows - 1, 0))
        for b, part in enumerate((before, lifted, after)):
            padded[:, 1 : height + 1, :, b * channels : (b + 1) * channels] = part.astype(
                jnp.bfloat16
            ).reshape(frames, height, width, channels)
        total = x
        for a in range(3):
            if first:
                load_ks(a).wait()
                for b in range(3):
                    scale(ks, 3 * a + b, s_s)
            total = total + jnp.dot(
                padded[:, a : a + height].reshape(rows, 3 * channels),
                ks[3 * a : 3 * a + 3].reshape(3 * channels, channels),
                preferred_element_type=jnp.float32,
            )
        mid = total.astype(jnp.bfloat16)
        middle[t] = mid
        ext[t, 1 : frames + 1] = silu(mid.astype(jnp.float32)).astype(jnp.bfloat16).reshape(
            frames, height, width, channels
        )

    def send_halo(t):
        @pl.when(has_right)
        def _():
            tail(t).start()

        @pl.when(has_left)
        def _():
            head(t).start()

    def temporal(t):
        def tap(j):
            return jnp.dot(
                ext[t, j : j + frames].reshape(rows, channels), kt[j],
                preferred_element_type=jnp.float32,
            )

        total = tap(1)

        @pl.when(has_left)
        def _():
            tail(t).wait_recv()

        total = total + tap(0)

        @pl.when(has_right)
        def _():
            head(t).wait_recv()

        total = total + tap(2)
        results[t] = (
            middle[t].astype(jnp.float32) + total.astype(jnp.bfloat16).astype(jnp.float32)
        ).astype(jnp.bfloat16).reshape(frames, height, width, channels)
        store(t).start()

    load_held().wait()
    spatial(0, True)
    pl.semaphore_wait(barrier, sum(there.astype(jnp.int32) for there, _ in neighbours))

    @pl.when(segment == 0)
    def _():
        send_halo(0)

    load_kt().wait()
    for j in range(3):
        scale(kt, j, s_t)

    def step(t, carry):
        @pl.when(segment == 0)
        def _():
            load_arrival(t).wait()

        @pl.when(has_up)
        def _():
            relay(t - 1).wait_recv()

            @pl.when(t == 1)
            def _():
                send_halo(0)

        spatial(t, False)
        late = (segment == 0) & (t == ticks - 1)

        @pl.when(jnp.logical_not(late))
        def _():
            send_halo(t)

        temporal(t - 1)

        @pl.when(has_down)
        def _():
            relay(t - 1).start()

        @pl.when(late)
        def _():
            send_halo(t)

        return carry

    lax.fori_loop(1, ticks, step, 0)
    temporal(ticks - 1)

    for t in range(ticks):
        store(t).wait()

        @pl.when(has_right)
        def _(t=t):
            tail(t).wait_send()

        @pl.when(has_left)
        def _(t=t):
            head(t).wait_send()

        if t < ticks - 1:
            @pl.when(has_down)
            def _(t=t):
                relay(t).wait_send()


def local(n_segment, n_seq, held, arrivals, w_s, s_s, w_t, s_t):
    ticks = arrivals.shape[0] + 1
    _, frames, height, width, channels = held.shape
    clip = (frames, height, width, channels)
    bf16, dma = jnp.bfloat16, pltpu.SemaphoreType.DMA
    hbm, vmem = pl.BlockSpec(memory_space=pl.ANY), pl.BlockSpec(memory_space=pltpu.VMEM)
    rows = frames * height * width
    return pl.pallas_call(
        functools.partial(kernel, n_segment, n_seq),
        out_shape=jax.ShapeDtypeStruct((1, ticks) + clip, bf16),
        in_specs=[hbm, hbm, hbm, vmem, hbm, vmem],
        out_specs=hbm,
        scratch_shapes=[
            pltpu.VMEM((ticks,) + clip, bf16),
            pltpu.VMEM((frames, height + 2, width, 3 * channels), bf16),
            pltpu.VMEM(w_s.shape[1:], bf16),
            pltpu.VMEM(w_t.shape[1:], bf16),
            pltpu.VMEM((ticks, rows, channels), bf16),
            pltpu.VMEM((ticks, frames + 2, height, width, channels), bf16),
            pltpu.VMEM((ticks,) + clip, bf16),
            dma((ticks,)), dma((3,)), dma, dma((ticks,)),
            dma((ticks,)), dma((ticks,)), dma((ticks, 2)), dma((ticks, 2)),
        ],
        compiler_params=pltpu.CompilerParams(
            collective_id=0, has_side_effects=True, vmem_limit_bytes=60 * 2**20
        ),
        cost_estimate=pl.CostEstimate(
            flops=2 * ticks * 12 * rows * channels * channels, bytes_accessed=2 * (w_s.size + w_t.size),
            transcendentals=0,
        ),
    )(held, arrivals, w_s, jnp.swapaxes(s_s, 0, 1), w_t, jnp.swapaxes(s_t, 0, 1))


def solution(mesh):
    in_specs = (
        P("segment", ("groups", "seq"), None, None, None),
        P(None, ("groups", "seq"), None, None, None),
        P("segment", None, None, None),
        P("segment", None, None),
        P("segment", None, None, None),
        P("segment", None, None),
    )
    out_specs = P("segment", None, ("groups", "seq"), None, None, None)
    body = functools.partial(local, mesh.shape["segment"], mesh.shape["seq"])
    return jax.shard_map(body, mesh=mesh, in_specs=in_specs, out_specs=out_specs, check_vma=False)
```

```python
import functools

import jax
import jax.numpy as jnp
from jax import lax
from jax.experimental import pallas as pl
from jax.experimental.pallas import tpu as pltpu
from jax.sharding import PartitionSpec as P

MESH = pl.DeviceIdType.MESH


def silu(v):
    return v / (1.0 + jnp.exp(-v))


def kernel(
    n_segment, n_seq,
    held, arrivals, w_s, s_s, w_t, s_t, out,
    clips, padded, ks, kt, middle, ext, results,
    clip_sem, ks_sem, kt_sem, out_sem, relay_send, relay_recv, halo_send, halo_recv,
):
    ticks, frames, height, width, channels = clips.shape
    rows = frames * height * width
    segment, seq = lax.axis_index("segment"), lax.axis_index("seq")
    has_left, has_right = seq > 0, seq < n_seq - 1
    has_up, has_down = segment > 0, segment < n_segment - 1
    neighbours = (
        (has_left, {"seq": seq - 1}),
        (has_right, {"seq": seq + 1}),
        (has_up, {"segment": segment - 1}),
        (has_down, {"segment": segment + 1}),
    )
    barrier = pltpu.get_barrier_semaphore()
    for there, where in neighbours:
        @pl.when(there)
        def _(where=where):
            pl.semaphore_signal(barrier, inc=1, device_id=where, device_id_type=MESH)

    def load_held():
        return pltpu.make_async_copy(held.at[0], clips.at[0], clip_sem.at[0])

    def load_arrival(t):
        return pltpu.make_async_copy(arrivals.at[t - 1], clips.at[t], clip_sem.at[t])

    def load_ks(row):
        return pltpu.make_async_copy(w_s.at[0, pl.ds(3 * row, 3)], ks.at[pl.ds(3 * row, 3)], ks_sem.at[row])

    def load_kt():
        return pltpu.make_async_copy(w_t.at[0], kt, kt_sem)

    def store(t):
        return pltpu.make_async_copy(results.at[t], out.at[0, t], out_sem.at[t])

    def relay(t):
        return pltpu.make_async_remote_copy(
            results.at[t], clips.at[t + 1], relay_send.at[t], relay_recv.at[t],
            device_id={"segment": segment + 1}, device_id_type=MESH,
        )

    def tail(t):
        return pltpu.make_async_remote_copy(
            ext.at[t, frames], ext.at[t, 0], halo_send.at[t, 0], halo_recv.at[t, 0],
            device_id={"seq": seq + 1}, device_id_type=MESH,
        )

    def head(t):
        return pltpu.make_async_remote_copy(
            ext.at[t, 1], ext.at[t, frames + 1], halo_send.at[t, 1], halo_recv.at[t, 1],
            device_id={"seq": seq - 1}, device_id_type=MESH,
        )

    load_held().start()
    for row in range(3):
        load_ks(row).start()
    load_kt().start()

    @pl.when(segment == 0)
    def _():
        for t in range(1, ticks):
            load_arrival(t).start()

    blank = jnp.zeros((frames, 1, width, 3 * channels), jnp.bfloat16)
    padded[:, 0:1] = blank
    padded[:, height + 1 : height + 2] = blank

    @pl.when(jnp.logical_not(has_left))
    def _():
        ext[:, 0] = jnp.zeros((ticks, height, width, channels), jnp.bfloat16)

    @pl.when(jnp.logical_not(has_right))
    def _():
        ext[:, frames + 1] = jnp.zeros((ticks, height, width, channels), jnp.bfloat16)

    def scale(kernels, tap, scales):
        blocks = scales.shape[0]
        block = channels // blocks
        for i in range(blocks):
            part = slice(i * block, (i + 1) * block)
            kernels[tap, part, :] = (
                kernels[tap, part, :].astype(jnp.float32) * scales[i]
            ).astype(jnp.bfloat16)

    def spatial(t, first):
        x = clips[t].reshape(rows, channels).astype(jnp.float32)
        lifted = silu(x)
        column = lax.broadcasted_iota(jnp.int32, (rows, channels), 0) % width
        before = jnp.where(column == 0, 0.0, pltpu.roll(lifted, 1, 0))
        after = jnp.where(column == width - 1, 0.0, pltpu.roll(lifted, rows - 1, 0))
        for b, part in enumerate((before, lifted, after)):
            padded[:, 1 : height + 1, :, b * channels : (b + 1) * channels] = part.astype(
                jnp.bfloat16
            ).reshape(frames, height, width, channels)
        total = x
        for a in range(3):
            if first:
                load_ks(a).wait()
                for b in range(3):
                    scale(ks, 3 * a + b, s_s)
            total = total + jnp.dot(
                padded[:, a : a + height].reshape(rows, 3 * channels),
                ks[3 * a : 3 * a + 3].reshape(3 * channels, channels),
                preferred_element_type=jnp.float32,
            )
        mid = total.astype(jnp.bfloat16)
        middle[t] = mid
        ext[t, 1 : frames + 1] = silu(mid.astype(jnp.float32)).astype(jnp.bfloat16).reshape(
            frames, height, width, channels
        )

    def send_halo(t):
        @pl.when(has_right)
        def _():
            tail(t).start()

        @pl.when(has_left)
        def _():
            head(t).start()

    def temporal(t):
        def tap(j):
            return jnp.dot(
                ext[t, j : j + frames].reshape(rows, channels), kt[j],
                preferred_element_type=jnp.float32,
            )

        total = tap(1)

        @pl.when(has_left)
        def _():
            tail(t).wait_recv()

        total = total + tap(0)

        @pl.when(has_right)
        def _():
            head(t).wait_recv()

        total = total + tap(2)
        results[t] = (
            middle[t].astype(jnp.float32) + total.astype(jnp.bfloat16).astype(jnp.float32)
        ).astype(jnp.bfloat16).reshape(frames, height, width, channels)
        store(t).start()

    load_held().wait()
    spatial(0, True)
    pl.semaphore_wait(barrier, sum(there.astype(jnp.int32) for there, _ in neighbours))

    @pl.when(segment == 0)
    def _():
        send_halo(0)

    load_kt().wait()
    for j in range(3):
        scale(kt, j, s_t)

    def step(t, carry):
        @pl.when(segment == 0)
        def _():
            load_arrival(t).wait()

        @pl.when(has_up)
        def _():
            relay(t - 1).wait_recv()

            @pl.when(t == 1)
            def _():
                send_halo(0)

        spatial(t, False)
        send_halo(t)
        temporal(t - 1)

        @pl.when(has_down)
        def _():
            relay(t - 1).start()

        return carry

    lax.fori_loop(1, ticks, step, 0)
    temporal(ticks - 1)

    for t in range(ticks):
        store(t).wait()

        @pl.when(has_right)
        def _(t=t):
            tail(t).wait_send()

        @pl.when(has_left)
        def _(t=t):
            head(t).wait_send()

        if t < ticks - 1:
            @pl.when(has_down)
            def _(t=t):
                relay(t).wait_send()


def local(n_segment, n_seq, held, arrivals, w_s, s_s, w_t, s_t):
    ticks = arrivals.shape[0] + 1
    _, frames, height, width, channels = held.shape
    clip = (frames, height, width, channels)
    bf16, dma = jnp.bfloat16, pltpu.SemaphoreType.DMA
    hbm, vmem = pl.BlockSpec(memory_space=pl.ANY), pl.BlockSpec(memory_space=pltpu.VMEM)
    rows = frames * height * width
    return pl.pallas_call(
        functools.partial(kernel, n_segment, n_seq),
        out_shape=jax.ShapeDtypeStruct((1, ticks) + clip, bf16),
        in_specs=[hbm, hbm, hbm, vmem, hbm, vmem],
        out_specs=hbm,
        scratch_shapes=[
            pltpu.VMEM((ticks,) + clip, bf16),
            pltpu.VMEM((frames, height + 2, width, 3 * channels), bf16),
            pltpu.VMEM(w_s.shape[1:], bf16),
            pltpu.VMEM(w_t.shape[1:], bf16),
            pltpu.VMEM((ticks, rows, channels), bf16),
            pltpu.VMEM((ticks, frames + 2, height, width, channels), bf16),
            pltpu.VMEM((ticks,) + clip, bf16),
            dma((ticks,)), dma((3,)), dma, dma((ticks,)),
            dma((ticks,)), dma((ticks,)), dma((ticks, 2)), dma((ticks, 2)),
        ],
        compiler_params=pltpu.CompilerParams(
            collective_id=0, has_side_effects=True, vmem_limit_bytes=60 * 2**20
        ),
        cost_estimate=pl.CostEstimate(
            flops=2 * ticks * 12 * rows * channels * channels, bytes_accessed=2 * (w_s.size + w_t.size),
            transcendentals=0,
        ),
    )(held, arrivals, w_s, jnp.swapaxes(s_s, 0, 1), w_t, jnp.swapaxes(s_t, 0, 1))


def solution(mesh):
    in_specs = (
        P("segment", ("groups", "seq"), None, None, None),
        P(None, ("groups", "seq"), None, None, None),
        P("segment", None, None, None),
        P("segment", None, None),
        P("segment", None, None, None),
        P("segment", None, None),
    )
    out_specs = P("segment", None, ("groups", "seq"), None, None, None)
    body = functools.partial(local, mesh.shape["segment"], mesh.shape["seq"])
    return jax.shard_map(body, mesh=mesh, in_specs=in_specs, out_specs=out_specs, check_vma=False)
```
